32 devices in a mesh: runs: 2 (over y), lat: 4 (over z), lon: 2 (over x), lev: 2 (over core).
Axes of the slice: x: 2, y: 2, z: 4, core: 2. Of those that a mesh axis runs over, the one named last changes fastest.
Arguments:
- northward_speed: float32 [32, 128, 1792], P(('runs', 'lev'), 'lat', 'lon'), parts along dimension 0, may hold values from -6 to 6
- thermal_anomaly: float32 [32, 128, 1792], P(('runs', 'lev'), 'lat', 'lon'), parts along dimension 0, may hold values from -6 to 6
- isopycnal_bucket: int32 [32, 128, 1792], P(('runs', 'lev'), 'lat', 'lon'), parts along dimension 0, may hold values from 0 to 95
- isopycnal_bucket_slot: float32 [32, 128, 1792], P(('runs', 'lev'), 'lat', 'lon'), parts along dimension 0, may hold values from 0 to 1
- profile_region_number: int32 [256, 1792], P(('runs', 'lat'), 'lon'), parts along dimension 0, may hold values from 0 to 2, as said below
- partition_sea_lines: int32 [8, 2, 32], P(('runs', 'lat'), 'lon'), parts along dimension 0, may hold values from 0 to 31, as said below
- partition_sea_numbers: int32 [8, 2], P('runs'), parts along dimension 0, may hold values from 1 to 32, as said below
Outputs:
- depth_heat: float32 [4, 2, 16, 128], P('runs', None, 'lev', 'lat'), parts along dimension 0
- class_heat: float32 [256, 12288], P(('runs', 'lat')), parts along dimension 0
The draws below stay inside these ranges and needn't reach their ends.
There are 2 independent parts, one for each index of `runs`. The reference program is written for one: setup_inputs(seed, part) draws one part's arguments, and reference() takes and returns one part's arrays. A program takes and returns all parts, laid end to end along the dimension named above; each array names one. Nothing has to cross between parts.
Inputs may be any that keep to these rules, and one draw needn't show every extreme that they name: `partition_sea_lines`: along the last dimension each device block's entries are its rows 0 to 31, each once. `partition_sea_numbers`: in every draw some device block lists all 32 of its rows. `profile_region_number`: 0 is Atlantic, 1 Indo-Pacific, 2 land; every column of a row that its device block does not list is land.
All inputs are finite; a program needn't handle non-finite values.
Results may differ from the reference program's by a relative error of at most 0.0003.
Values sent between devices are 32-bit elements; how exact they have to be, the bound alone decides.
A program may use at most 128 MiB of HBM per device.

```python
import math
import jax
import jax.numpy as jnp
from jax import lax

RY = 32
CX = 896
CLS = 96
TCLS = 32
NB = 2
QTY = 4
VERTICAL_LAYERS = 16
NORTHING_LINES = 128
EASTING_POINTS = 1792
BANDS = 4
GROUPS = 2


def wet_plan(key):
    count_key, full_key, order_key = jax.random.split(key, 3)
    devices = BANDS * GROUPS
    grid_point_numbers = jax.random.randint(count_key, (devices,), 2, RY // 2 + 1)
    full_device = jax.random.randint(full_key, (), 0, devices)
    grid_point_numbers = jnp.where(jnp.arange(devices) == full_device, RY, grid_point_numbers)
    orders = jax.vmap(lambda sub_key: jax.random.permutation(sub_key, RY))(jax.random.split(order_key, devices))
    return (grid_point_numbers.reshape(BANDS, GROUPS).astype(jnp.int32), orders.reshape(BANDS, GROUPS, RY).astype(jnp.int32))


def draw_partition_sea_lines(key, part):
    grid_point_numbers, orders = wet_plan(key)
    return orders


def draw_partition_sea_numbers(key, part):
    grid_point_numbers, orders = wet_plan(key)
    return grid_point_numbers


def draw_profile_region_number(key, part):
    grid_point_numbers, orders = wet_plan(key)
    key = jax.random.fold_in(key, 7)
    atlantic_key, pacific_key, absent_key = jax.random.split(key, 3)
    atlantic = jax.random.randint(atlantic_key, (NORTHING_LINES, 1), 0, EASTING_POINTS // 2)
    absent = jax.random.randint(absent_key, (NORTHING_LINES, 1), 0, 4)
    atlantic = jnp.where(absent == 0, 0, atlantic)
    pacific = atlantic + jax.random.randint(pacific_key, (NORTHING_LINES, 1), EASTING_POINTS // 4, EASTING_POINTS // 2 + 1)
    columns = jnp.arange(EASTING_POINTS)[None, :]
    basins = jnp.where(columns < atlantic, 0, jnp.where(columns < pacific, 1, 2))
    positions = jnp.arange(RY)
    row_ranks = jnp.sum((orders[:, :, :, None] == positions[None, None, None, :]) * jnp.arange(RY)[None, None, :, None], axis=2)
    enumerated_lines = row_ranks < grid_point_numbers[:, :, None]
    enumerated_lines = jnp.repeat(jnp.transpose(enumerated_lines, (0, 2, 1)).reshape(NORTHING_LINES, GROUPS), CX, axis=1)
    return jnp.where(enumerated_lines, basins, 2).astype(jnp.int32)


def touch_ends(values, rng, smallest, high):
    longest = values.shape.index(max(values.shape))
    spots = []
    for shift in (0, 1):
        where = [jax.random.randint(jax.random.fold_in(rng, axis), (), 0, length) for axis, length in enumerate(values.shape)]
        where[longest] = (where[longest] + shift) % values.shape[longest]
        spots.append(tuple(where))
    return values.at[spots[0]].set(smallest).at[spots[1]].set(high)


def steps_of(own_key, extent, cuts, smallest, largest):
    loudness, own = 1.0, jax.random.fold_in(own_key, 6)
    for axis_at, shards_of in cuts:
        heights = jnp.exp(jax.random.uniform(jax.random.fold_in(own, axis_at), (shards_of,), jnp.float32, smallest / len(cuts), largest / len(cuts)))
        loudness = loudness * jnp.repeat(heights, extent[axis_at] // shards_of).reshape([-1 if axis == axis_at else 1 for axis in range(len(extent))])
    return loudness


def scatter_about(rng, dims, width, bound, pieces=(), held_as=jnp.bfloat16):
    array = width * jax.random.normal(rng, dims, jnp.float32)
    if pieces:
        array = array * steps_of(rng, dims, pieces, -0.22, 0.18)
    return jnp.clip(array, -bound, bound).astype(held_as)


def setup_inputs(seed: int = 0, part: int = 0) -> dict:
    arg_keys = jax.random.split(jax.random.key(seed), 8)
    own_keys = jax.random.split(jax.random.fold_in(arg_keys[7], part), 8)
    return {
        "northward_speed": scatter_about(own_keys[0], (VERTICAL_LAYERS, NORTHING_LINES, EASTING_POINTS), 1.0, 6.0, ((0, 2), (1, 4), (2, 2)), jnp.float32),
        "thermal_anomaly": scatter_about(own_keys[1], (VERTICAL_LAYERS, NORTHING_LINES, EASTING_POINTS), 1.0, 6.0, ((0, 2), (1, 4), (2, 2)), jnp.float32),
        "isopycnal_bucket": touch_ends(jax.random.randint(own_keys[2], (VERTICAL_LAYERS, NORTHING_LINES, EASTING_POINTS), 0, CLS), jax.random.fold_in(own_keys[2], 1), 0, CLS - 1).astype(jnp.int32),
        "isopycnal_bucket_slot": jnp.clip(1.0 * jax.random.uniform(own_keys[3], (VERTICAL_LAYERS, NORTHING_LINES, EASTING_POINTS), jnp.float32) ** steps_of(own_keys[3], (VERTICAL_LAYERS, NORTHING_LINES, EASTING_POINTS), ((0, 2), (1, 4), (2, 2)), -0.2, 0.2), 0.0, 1.0),
        "profile_region_number": draw_profile_region_number(jax.random.fold_in(jax.random.fold_in(arg_keys[7], part), 71), part),
        "partition_sea_lines": draw_partition_sea_lines(jax.random.fold_in(jax.random.fold_in(arg_keys[7], part), 71), part),
        "partition_sea_numbers": draw_partition_sea_numbers(jax.random.fold_in(jax.random.fold_in(arg_keys[7], part), 71), part),
    }


def eastwest_parts(northward_accumulated, thermal_accumulated, accumulated_covariance, grid_point_numbers):
    averaging_denominator = jnp.maximum(grid_point_numbers, 1.0)[:, None, :]
    northward_average = northward_accumulated / averaging_denominator
    thermal_average = thermal_accumulated / averaging_denominator
    meridional_circulation_part = northward_accumulated * thermal_accumulated / averaging_denominator
    stationary_eddy_part = (accumulated_covariance - meridional_circulation_part) / math.sqrt(EASTING_POINTS)
    return (northward_average, thermal_average, meridional_circulation_part, stationary_eddy_part)

def reference(northward_speed, thermal_anomaly, isopycnal_bucket, isopycnal_bucket_slot, profile_region_number, partition_sea_lines, partition_sea_numbers):
    basins = jnp.arange(NB, dtype=jnp.int32)
    ocean_region_filters = (profile_region_number[None, :, :] == basins[:, None, None]).astype(jnp.float32)
    grid_point_numbers = lax.optimization_barrier(jnp.sum(ocean_region_filters, axis=-1))
    northward_filtered = ocean_region_filters[:, None] * northward_speed[None]
    northward_accumulated = lax.optimization_barrier(jnp.sum(northward_filtered, axis=-1))
    thermal_accumulated = lax.optimization_barrier(jnp.sum(ocean_region_filters[:, None] * thermal_anomaly[None], axis=-1))
    accumulated_covariance = lax.optimization_barrier(jnp.sum(northward_filtered * thermal_anomaly[None], axis=-1))
    northward_average, thermal_average, meridional_circulation_part, stationary_eddy_part = eastwest_parts(northward_accumulated, thermal_accumulated, accumulated_covariance, grid_point_numbers)
    depth_heat = jnp.stack([meridional_circulation_part, stationary_eddy_part])
    positions = jnp.arange(RY, dtype=jnp.int32)
    placed = partition_sea_lines[:, :, :, None] == positions[None, None, None, :]
    place_index = jnp.arange(RY, dtype=jnp.int32)[None, None, :, None]
    enumerated_lines = jnp.any(placed & (place_index < partition_sea_numbers[:, :, None, None]), axis=2)
    enumerated_lines = jnp.transpose(enumerated_lines, (0, 2, 1)).reshape(NORTHING_LINES, GROUPS)
    enumerated_lines = jnp.repeat(enumerated_lines, CX, axis=1).astype(jnp.float32)
    volume = northward_filtered * enumerated_lines
    thermal_transport_piece = ocean_region_filters[:, None] * (northward_speed[None] - northward_average[..., None]) * (thermal_anomaly[None] - thermal_average[..., None]) * enumerated_lines
    features = jnp.concatenate([volume, thermal_transport_piece], 0)
    class_pos = jnp.minimum(isopycnal_bucket.astype(jnp.float32) + isopycnal_bucket_slot, CLS - 1.0)
    temp_pos = jnp.minimum(jnp.maximum((thermal_anomaly + 3.0) * (TCLS / 6.0), 0.0), TCLS - 1.0)
    classes = jnp.arange(CLS, dtype=jnp.float32)
    temp_classes = jnp.arange(TCLS, dtype=jnp.float32)

    def one_row(row_inputs):
        feature_row, pos_row, temp_row = row_inputs
        tent_weights = jnp.maximum(0.0, 1.0 - jnp.abs(pos_row.reshape(1, -1) - classes[:, None]))
        temp_weights = jnp.maximum(0.0, 1.0 - jnp.abs(temp_row.reshape(1, -1) - temp_classes[:, None]))
        weighted = (feature_row.reshape(QTY, 1, -1) * temp_weights[None]).reshape(QTY * TCLS, -1)
        class_binned_heat = lax.dot_general(weighted, tent_weights, (((1,), (1,)), ((), ())), precision=lax.Precision.HIGHEST)
        return class_binned_heat.reshape(-1)
    row_sums = lax.map(one_row, (jnp.moveaxis(features, 2, 0), jnp.moveaxis(class_pos, 1, 0), jnp.moveaxis(temp_pos, 1, 0)))
    class_heat = row_sums / math.sqrt(VERTICAL_LAYERS * EASTING_POINTS / (CLS * TCLS))
    return (depth_heat, class_heat)
```

```python
import functools
import math

import jax
import jax.numpy as jnp
from jax import lax
from jax.experimental import pallas as pl
from jax.experimental.pallas import tpu as pltpu
from jax.sharding import PartitionSpec as P

CLS = 96
TCLS = 32
NB = 2
BT = NB * TCLS
QT = 2 * BT
F32 = jnp.float32
BF16 = jnp.bfloat16


def split(x):
    high = x.astype(BF16).astype(F32)
    return high, x - high


def prepare(k, v, t, bucket, slot, basin, means, rows_ref):
    position = jnp.minimum(bucket.astype(F32) + slot, CLS - 1.0)
    cls = jnp.floor(position)
    upper = position - cls
    temp_pos = jnp.minimum(jnp.maximum((t + 3.0) * (TCLS / 6.0), 0.0), TCLS - 1.0)
    temp = jnp.floor(temp_pos)
    warm = temp_pos - temp
    cold = 1.0 - warm
    first = basin == 0
    second = basin == 1
    mean_v = jnp.where(first, means[0], means[1])
    mean_t = jnp.where(first, means[2], means[3])
    eddy = (v - mean_v) * (t - mean_t)
    joint = jnp.where(first, temp, jnp.where(second, temp + TCLS, -128.0))
    values = [cls, *split(1.0 - upper), *split(upper), joint]
    for feature in (v, eddy):
        values += [*split(feature * cold), *split(feature * warm)]
    for slot_at, value in enumerate(values):
        rows_ref[slot_at, k] = value


def bin_row(y, rows_ref, levels, columns, scale):
    spots = lax.broadcasted_iota(jnp.int32, (16, columns), 0).astype(F32)
    total = None
    step = 2 if levels % 2 == 0 else 1
    for k0 in range(0, levels, step):
        tents, weights = [], []
        for k in range(k0, k0 + step):
            def row(at):
                return jnp.broadcast_to(rows_ref[at, k, pl.ds(y, 1), :], (16, columns)).astype(BF16)

            zero = jnp.zeros((16, columns), BF16)
            cls, low_hi, low_lo, up_hi, up_lo, joint = [row(at) for at in range(6)]
            feats = [row(at) for at in range(6, 14)]
            tent_hi, tent_lo = [], []
            for c in range(0, CLS, 16):
                here = (spots + float(c)).astype(BF16)
                before = (spots + float(c - 1)).astype(BF16)
                at_low = cls == here
                at_up = cls == before
                tent_hi.append(jnp.where(at_low, low_hi, jnp.where(at_up, up_hi, zero)))
                tent_lo.append(jnp.where(at_low, low_lo, jnp.where(at_up, up_lo, zero)))
            blocks = [[], [], [], []]
            for c in range(0, BT, 16):
                here = (spots + float(c)).astype(BF16)
                before = (spots + float(c - 1)).astype(BF16)
                at_low = joint == here
                at_up = joint == before
                for n, (kind, part) in enumerate(((0, 0), (1, 0), (0, 1), (1, 1))):
                    low = feats[4 * kind + part]
                    up = feats[4 * kind + 2 + part]
                    blocks[n].append(jnp.where(at_low, low, jnp.where(at_up, up, zero)))
            tents.append(jnp.concatenate(tent_hi + tent_lo, 0))
            weights.append(jnp.concatenate(sum(blocks, []), 0))
        product = lax.dot_general(
            jnp.concatenate(tents, 1),
            jnp.concatenate(weights, 1),
            (((1,), (1,)), ((), ())),
            preferred_element_type=F32,
        )
        total = product if total is None else total + product
    total = total[:, :QT] + total[:, QT:]
    return (total[:CLS] + total[CLS:]) * scale


def bin_kernel(scale, v_ref, t_ref, bucket_ref, slot_ref, basin_ref, means_ref, out_ref, rows_ref, sums_ref):
    levels, row_count, columns = v_ref.shape
    basin = basin_ref[...]
    for k in range(levels):
        means = [means_ref[:, 4 * k + n : 4 * k + n + 1] for n in range(4)]
        prepare(k, v_ref[k], t_ref[k], bucket_ref[k], slot_ref[k], basin, means, rows_ref)

    def one_row(y, carry):
        binned = bin_row(y, rows_ref, levels, columns, scale)
        binned = jnp.concatenate([binned, jnp.zeros((128 - CLS, QT), F32)], 0)
        sums_ref[pl.ds(y, QT, stride=row_count), :] = binned.T
        return carry

    lax.fori_loop(0, row_count, one_row, 0)

    def flatten(group, carry):
        parts = []
        for m in range(4):
            start = pl.multiple_of((group * 4 + m) * row_count, row_count)
            parts.append(sums_ref[pl.ds(start, row_count), :][:, :CLS])
        out_ref[:, pl.ds(pl.multiple_of(group * (4 * CLS), 128), 4 * CLS)] = jnp.concatenate(parts, 1)
        return carry

    lax.fori_loop(0, QT // 4, flatten, 0)


def shards(
    northward_speed,
    thermal_anomaly,
    isopycnal_bucket,
    isopycnal_bucket_slot,
    profile_region_number,
    partition_sea_lines,
    partition_sea_numbers,
):
    levels, row_count, columns = northward_speed.shape
    zonal_width = columns * lax.axis_size("lon")
    level_count = levels * lax.axis_size("lev")
    basins = jnp.arange(NB, dtype=jnp.int32)
    masks = (profile_region_number[None] == basins[:, None, None]).astype(F32)
    filtered = masks[:, None] * northward_speed[None]
    stacked = jnp.stack(
        [
            jnp.sum(filtered, -1),
            jnp.sum(masks[:, None] * thermal_anomaly[None], -1),
            jnp.sum(filtered * thermal_anomaly[None], -1),
        ]
    )
    sums, counts = lax.psum((stacked, jnp.sum(masks, -1)), "lon")
    divisor = jnp.maximum(counts, 1.0)[:, None, :]
    means = sums[:2] / divisor
    overturning = sums[0] * sums[1] / divisor
    eddy = (sums[2] - overturning) / math.sqrt(zonal_width)
    depth_heat = jnp.stack([overturning, eddy])
    own_count = partition_sea_numbers[lax.axis_index("lat"), lax.axis_index("lon")]
    lines = partition_sea_lines[0, 0]
    places = jnp.arange(row_count, dtype=jnp.int32)
    listed = jnp.any((lines[None, :] == places[:, None]) & (places[None, :] < own_count), 1)
    basin = jnp.where(listed[:, None], profile_region_number, NB)
    means = jnp.transpose(means, (3, 2, 0, 1)).reshape(row_count, levels * 4)
    means = jnp.pad(means, ((0, 0), (0, 128 - levels * 4)))
    scale = 1.0 / math.sqrt(level_count * zonal_width / (CLS * TCLS))
    vmem = pl.BlockSpec(memory_space=pltpu.VMEM)
    binned = pl.pallas_call(
        functools.partial(bin_kernel, scale),
        out_shape=jax.ShapeDtypeStruct((row_count, QT * CLS), F32),
        in_specs=[vmem] * 6,
        out_specs=vmem,
        scratch_shapes=[
            pltpu.VMEM((14, levels, row_count, columns), F32),
            pltpu.VMEM((QT * row_count, 128), F32),
        ],
        compiler_params=pltpu.CompilerParams(vmem_limit_bytes=48 * 1024 * 1024),
    )(northward_speed, thermal_anomaly, isopycnal_bucket, isopycnal_bucket_slot, basin, means)
    return depth_heat, lax.psum(binned, ("lon", "lev"))


def solution(mesh):
    in_specs = (
        P(("runs", "lev"), "lat", "lon"),
        P(("runs", "lev"), "lat", "lon"),
        P(("runs", "lev"), "lat", "lon"),
        P(("runs", "lev"), "lat", "lon"),
        P(("runs", "lat"), "lon"),
        P(("runs", "lat"), "lon", None),
        P("runs", None),
    )
    out_specs = (P("runs", None, "lev", "lat"), P(("runs", "lat"), None))
    return jax.shard_map(shards, mesh=mesh, in_specs=in_specs, out_specs=out_specs, check_vma=False)
```

```python
import functools
import math

import jax
import jax.numpy as jnp
from jax import lax
from jax.experimental import pallas as pl
from jax.experimental.pallas import tpu as pltpu
from jax.sharding import PartitionSpec as P

CLS = 96
TCLS = 32
NB = 2
BT = NB * TCLS
QT = 2 * BT
F32 = jnp.float32
BF16 = jnp.bfloat16


def split(x):
    high = x.astype(BF16).astype(F32)
    return high, x - high


ROWS = 8
STATS = 8


def temperature(t):
    temp_pos = jnp.minimum(jnp.maximum((t + 3.0) * (TCLS / 6.0), 0.0), TCLS - 1.0)
    temp = jnp.floor(temp_pos)
    return temp, temp_pos - temp


def prepare_classes(k, v, t, bucket, slot, listed_basin, rows_ref):
    position = jnp.minimum(bucket.astype(F32) + slot, CLS - 1.0)
    cls = jnp.floor(position)
    upper = position - cls
    temp, warm = temperature(t)
    joint = jnp.where(
        listed_basin == 0, temp, jnp.where(listed_basin == 1, temp + TCLS, -128.0)
    )
    values = [cls, *split(1.0 - upper), *split(upper), joint]
    values += [*split(v * (1.0 - warm)), *split(v * warm)]
    for at, value in enumerate(values):
        rows_ref[at, k] = value


def prepare_eddies(k, v, t, listed_basin, means, rows_ref):
    first = listed_basin == 0
    eddy = (v - jnp.where(first, means[0], means[1])) * (t - jnp.where(first, means[2], means[3]))
    _, warm = temperature(t)
    for at, value in enumerate([*split(eddy * (1.0 - warm)), *split(eddy * warm)]):
        rows_ref[10 + at, k] = value


def bin_row(y, rows_ref, levels, columns, scale):
    spots = lax.broadcasted_iota(jnp.int32, (16, columns), 0).astype(F32)
    total = None
    step = 2 if levels % 2 == 0 else 1
    for k0 in range(0, levels, step):
        tents, weights = [], []
        for k in range(k0, k0 + step):
            def row(at):
                return jnp.broadcast_to(rows_ref[at, k, pl.ds(y, 1), :], (16, columns)).astype(BF16)

            zero = jnp.zeros((16, columns), BF16)
            cls, low_hi, low_lo, up_hi, up_lo, joint = [row(at) for at in range(6)]
            feats = [row(at) for at in range(6, 14)]
            tent_hi, tent_lo = [], []
            for c in range(0, CLS, 16):
                here = (spots + float(c)).astype(BF16)
                before = (spots + float(c - 1)).astype(BF16)
                at_low = cls == here
                at_up = cls == before
                tent_hi.append(jnp.where(at_low, low_hi, jnp.where(at_up, up_hi, zero)))
                tent_lo.append(jnp.where(at_low, low_lo, jnp.where(at_up, up_lo, zero)))
            blocks = [[], [], [], []]
            for c in range(0, BT, 16):
                here = (spots + float(c)).astype(BF16)
                before = (spots + float(c - 1)).astype(BF16)
                at_low = joint == here
                at_up = joint == before
                for n, (kind, part) in enumerate(((0, 0), (1, 0), (0, 1), (1, 1))):
                    low = feats[4 * kind + part]
                    up = feats[4 * kind + 2 + part]
                    blocks[n].append(jnp.where(at_low, low, jnp.where(at_up, up, zero)))
            tents.append(jnp.concatenate(tent_hi + tent_lo, 0))
            weights.append(jnp.concatenate(sum(blocks, []), 0))
        product = lax.dot_general(
            jnp.concatenate(tents, 1),
            jnp.concatenate(weights, 1),
            (((1,), (1,)), ((), ())),
            preferred_element_type=F32,
        )
        total = product if total is None else total + product
    total = total[:, :QT] + total[:, QT:]
    return (total[:CLS] + total[CLS:]) * scale


def kernel(
    lon_size,
    zonal_width,
    scale,
    v_ref,
    t_ref,
    bucket_ref,
    slot_ref,
    basin_ref,
    lines_ref,
    numbers_ref,
    depth_ref,
    out_ref,
    rows_ref,
    sums_ref,
    stats_ref,
    part_ref,
    core_ref,
    lons_ref,
    stats_send,
    stats_recv,
    core_send,
    core_recv,
    lon_send,
    lon_recv,
    last_send,
    last_recv,
):
    levels, row_count, columns = v_ref.shape
    chunks = row_count // ROWS
    half = QT * CLS // 2
    lat = lax.axis_index("lat")
    lon = lax.axis_index("lon")
    lev = lax.axis_index("lev")
    other = 1 - lev
    mesh_id = pl.DeviceIdType.MESH

    barrier = pltpu.get_barrier_semaphore()
    pl.semaphore_signal(barrier, inc=1, device_id={"lev": other}, device_id_type=mesh_id)
    for d in range(1, lon_size):
        pl.semaphore_signal(
            barrier, inc=1, device_id={"lon": lax.rem(lon + d, lon_size)}, device_id_type=mesh_id
        )

    basin = basin_ref[...]
    lane = lax.broadcasted_iota(jnp.int32, (row_count, 128), 1)
    packed = jnp.zeros((row_count, 128), F32)
    for b in range(NB):
        mask = (basin == b).astype(F32)
        count = jnp.sum(mask, -1, keepdims=True)
        packed = jnp.where(lane == STATS * levels + b, count, packed)
        for k in range(levels):
            filtered = mask * v_ref[k]
            t = t_ref[k]
            for n, value in enumerate((filtered, mask * t, filtered * t)):
                total = jnp.sum(value, -1, keepdims=True)
                packed = jnp.where(lane == STATS * k + 2 * n + b, total, packed)
    stats_ref[lon] = packed

    pl.semaphore_wait(barrier, lon_size)

    def stats_copy(d):
        return pltpu.make_async_remote_copy(
            src_ref=stats_ref.at[lon],
            dst_ref=stats_ref.at[lon],
            send_sem=stats_send.at[d - 1],
            recv_sem=stats_recv.at[d - 1],
            device_id={"lon": lax.rem(lon + d, lon_size)},
            device_id_type=mesh_id,
        )

    for d in range(1, lon_size):
        stats_copy(d).start()

    numbers = numbers_ref[...]
    spot = (lax.broadcasted_iota(jnp.int32, numbers.shape, 0) == lat) & (
        lax.broadcasted_iota(jnp.int32, numbers.shape, 1) == lon
    )
    own = jnp.sum(jnp.where(spot, numbers.astype(F32), 0.0), -1, keepdims=True)
    own = jnp.sum(own, 0, keepdims=True)
    lines = lines_ref[...]
    square = (row_count, row_count)
    place = lax.broadcasted_iota(jnp.int32, square, 1).astype(F32)
    line = lax.broadcasted_iota(jnp.int32, square, 0)
    hit = jnp.where((line == lines) & (place < own), 1.0, 0.0)
    listed = jnp.max(hit, -1, keepdims=True)
    listed_basin = jnp.where(listed > 0.5, basin, NB)

    for k in range(levels):
        prepare_classes(k, v_ref[k], t_ref[k], bucket_ref[k], slot_ref[k], listed_basin, rows_ref)

    for d in range(1, lon_size):
        stats_copy(d).wait()
    stats = stats_ref[0]
    for n in range(1, lon_size):
        stats = stats + stats_ref[n]

    depth = jnp.zeros((row_count, 128), F32)
    divisors = [
        jnp.maximum(stats[:, STATS * levels + b : STATS * levels + b + 1], 1.0) for b in range(NB)
    ]
    for k in range(levels):
        means = []
        for n in range(2):
            for b in range(NB):
                at = STATS * k + 2 * n + b
                means.append(stats[:, at : at + 1] / divisors[b])
        for b in range(NB):
            at = STATS * k + b
            overturning = stats[:, at : at + 1] * stats[:, at + 2 : at + 3] / divisors[b]
            eddy = (stats[:, at + 4 : at + 5] - overturning) / math.sqrt(zonal_width)
            depth = jnp.where(lane == b * levels + k, overturning, depth)
            depth = jnp.where(lane == (NB + b) * levels + k, eddy, depth)
        prepare_eddies(k, v_ref[k], t_ref[k], listed_basin, means, rows_ref)
    turned = depth.T
    for n in range(2):
        for b in range(NB):
            at = (n * NB + b) * levels
            depth_ref[n, b] = turned[at : at + levels]

    def core_copy(i):
        return pltpu.make_async_remote_copy(
            src_ref=part_ref.at[i, other],
            dst_ref=core_ref.at[i],
            send_sem=core_send.at[i],
            recv_sem=core_recv.at[i],
            device_id={"lev": other},
            device_id_type=mesh_id,
        )

    def lon_copy(i, d):
        return pltpu.make_async_remote_copy(
            src_ref=lons_ref.at[lon, i],
            dst_ref=lons_ref.at[lon, i],
            send_sem=lon_send.at[i, d - 1],
            recv_sem=lon_recv.at[i, d - 1],
            device_id={"lon": lax.rem(lon + d, lon_size)},
            device_id_type=mesh_id,
        )

    def out_block(i):
        rows = pl.ds(pl.multiple_of(i * ROWS, ROWS), ROWS)
        return out_ref.at[rows, pl.ds(pl.multiple_of(lev * half, 128), half)]

    def last_copy(i):
        return pltpu.make_async_remote_copy(
            src_ref=out_block(i),
            dst_ref=out_block(i),
            send_sem=last_send.at[i],
            recv_sem=last_recv.at[i],
            device_id={"lev": other},
            device_id_type=mesh_id,
        )

    def over_cores(i):
        core_copy(i).wait_recv()
        lons_ref[lon, i] = part_ref[i, lev] + core_ref[i]
        for d in range(1, lon_size):
            lon_copy(i, d).start()

    def over_lons(i):
        for d in range(1, lon_size):
            lon_copy(i, d).wait_recv()
        total = lons_ref[0, i]
        for n in range(1, lon_size):
            total = total + lons_ref[n, i]
        out_block(i)[...] = total
        last_copy(i).start()

    def one_chunk(i, carry):
        def one_row(r, inner):
            binned = bin_row(i * ROWS + r, rows_ref, levels, columns, scale)
            binned = jnp.concatenate([binned, jnp.zeros((128 - CLS, QT), F32)], 0)
            sums_ref[pl.ds(r, QT, stride=ROWS), :] = binned.T
            return inner

        lax.fori_loop(0, ROWS, one_row, 0)

        def flatten(group, inner):
            for h in range(2):
                parts = []
                for m in range(4):
                    start = pl.multiple_of((h * (QT // 2) + group * 4 + m) * ROWS, ROWS)
                    parts.append(sums_ref[pl.ds(start, ROWS), :][:, :CLS])
                where = pl.ds(pl.multiple_of(group * (4 * CLS), 128), 4 * CLS)
                part_ref[i, h, :, where] = jnp.concatenate(parts, 1)
            return inner

        lax.fori_loop(0, QT // 8, flatten, 0)
        core_copy(i).start()

        @pl.when(i >= 1)
        def _():
            over_lons(i - 1)

        over_cores(i)
        return carry

    lax.fori_loop(0, chunks, one_chunk, 0)
    over_lons(chunks - 1)

    def finish(i, carry):
        core_copy(i).wait_send()
        for d in range(1, lon_size):
            lon_copy(i, d).wait_send()
        last_copy(i).wait()
        return carry

    lax.fori_loop(0, chunks, finish, 0)


def shards(
    northward_speed,
    thermal_anomaly,
    isopycnal_bucket,
    isopycnal_bucket_slot,
    profile_region_number,
    partition_sea_lines,
    partition_sea_numbers,
):
    levels, row_count, columns = northward_speed.shape
    lon_size = lax.axis_size("lon")
    zonal_width = columns * lon_size
    level_count = levels * lax.axis_size("lev")
    chunks = row_count // ROWS
    half = QT * CLS // 2
    scale = 1.0 / math.sqrt(level_count * zonal_width / (CLS * TCLS))
    vmem = pl.BlockSpec(memory_space=pltpu.VMEM)
    dma = pltpu.SemaphoreType.DMA
    return pl.pallas_call(
        functools.partial(kernel, lon_size, zonal_width, scale),
        out_shape=(
            jax.ShapeDtypeStruct((2, NB, levels, row_count), F32),
            jax.ShapeDtypeStruct((row_count, QT * CLS), F32),
        ),
        in_specs=[vmem] * 7,
        out_specs=(vmem, vmem),
        scratch_shapes=[
            pltpu.VMEM((14, levels, row_count, columns), F32),
            pltpu.VMEM((QT * ROWS, 128), F32),
            pltpu.VMEM((lon_size, row_count, 128), F32),
            pltpu.VMEM((chunks, 2, ROWS, half), F32),
            pltpu.VMEM((chunks, ROWS, half), F32),
            pltpu.VMEM((lon_size, chunks, ROWS, half), F32),
            dma((lon_size - 1,)),
            dma((lon_size - 1,)),
            dma((chunks,)),
            dma((chunks,)),
            dma((chunks, lon_size - 1)),
            dma((chunks, lon_size - 1)),
            dma((chunks,)),
            dma((chunks,)),
        ],
        compiler_params=pltpu.CompilerParams(
            collective_id=0, has_side_effects=True, vmem_limit_bytes=48 * 1024 * 1024
        ),
    )(
        northward_speed,
        thermal_anomaly,
        isopycnal_bucket,
        isopycnal_bucket_slot,
        profile_region_number,
        partition_sea_lines.reshape(1, row_count),
        partition_sea_numbers,
    )


def solution(mesh):
    in_specs = (
        P(("runs", "lev"), "lat", "lon"),
        P(("runs", "lev"), "lat", "lon"),
        P(("runs", "lev"), "lat", "lon"),
        P(("runs", "lev"), "lat", "lon"),
        P(("runs", "lat"), "lon"),
        P(("runs", "lat"), "lon", None),
        P("runs", None),
    )
    out_specs = (P("runs", None, "lev", "lat"), P(("runs", "lat"), None))
    return jax.shard_map(shards, mesh=mesh, in_specs=in_specs, out_specs=out_specs, check_vma=False)
```

```python
import functools
import math

import jax
import jax.numpy as jnp
from jax import lax
from jax.experimental import pallas as pl
from jax.experimental.pallas import tpu as pltpu
from jax.sharding import PartitionSpec as P

CLS = 96
TCLS = 32
NB = 2
BT = NB * TCLS
QT = 2 * BT
F32 = jnp.float32
BF16 = jnp.bfloat16


def split(x):
    high = x.astype(BF16).astype(F32)
    return high, x - high


ROWS = 8
STATS = 8
UNROLL = 2


def temperature(t):
    temp_pos = jnp.minimum(jnp.maximum((t + 3.0) * (TCLS / 6.0), 0.0), TCLS - 1.0)
    temp = jnp.floor(temp_pos)
    return temp, temp_pos - temp


def prepare_classes(k, v, t, bucket, slot, listed_basin, rows_ref):
    position = jnp.minimum(bucket.astype(F32) + slot, CLS - 1.0)
    cls = jnp.floor(position)
    upper = position - cls
    temp, warm = temperature(t)
    joint = jnp.where(
        listed_basin == 0, temp, jnp.where(listed_basin == 1, temp + TCLS, -128.0)
    )
    values = [cls, *split(1.0 - upper), *split(upper), joint]
    values += [*split(v * (1.0 - warm)), *split(v * warm)]
    for at, value in enumerate(values):
        rows_ref[at, k] = value


def prepare_eddies(k, v, t, listed_basin, means, rows_ref):
    first = listed_basin == 0
    eddy = (v - jnp.where(first, means[0], means[1])) * (t - jnp.where(first, means[2], means[3]))
    _, warm = temperature(t)
    for at, value in enumerate([*split(eddy * (1.0 - warm)), *split(eddy * warm)]):
        rows_ref[10 + at, k] = value


def bin_row(y, rows_ref, levels, columns, scale):
    spots = lax.broadcasted_iota(jnp.int32, (16, columns), 0).astype(F32)
    total = None
    step = 2 if levels % 2 == 0 else 1
    for k0 in range(0, levels, step):
        tents, weights = [], []
        for k in range(k0, k0 + step):
            def row(at):
                return jnp.broadcast_to(rows_ref[at, k, pl.ds(y, 1), :], (16, columns)).astype(BF16)

            zero = jnp.zeros((16, columns), BF16)
            cls, low_hi, low_lo, up_hi, up_lo, joint = [row(at) for at in range(6)]
            feats = [row(at) for at in range(6, 14)]
            tent_hi, tent_lo = [], []
            for c in range(0, CLS, 16):
                here = (spots + float(c)).astype(BF16)
                before = (spots + float(c - 1)).astype(BF16)
                at_low = cls == here
                at_up = cls == before
                tent_hi.append(jnp.where(at_low, low_hi, jnp.where(at_up, up_hi, zero)))
                tent_lo.append(jnp.where(at_low, low_lo, jnp.where(at_up, up_lo, zero)))
            blocks = [[], [], [], []]
            for c in range(0, BT, 16):
                here = (spots + float(c)).astype(BF16)
                before = (spots + float(c - 1)).astype(BF16)
                at_low = joint == here
                at_up = joint == before
                for n, (kind, part) in enumerate(((0, 0), (1, 0), (0, 1), (1, 1))):
                    low = feats[4 * kind + part]
                    up = feats[4 * kind + 2 + part]
                    blocks[n].append(jnp.where(at_low, low, jnp.where(at_up, up, zero)))
            tents.append(jnp.concatenate(tent_hi + tent_lo, 0))
            weights.append(jnp.concatenate(sum(blocks, []), 0))
        product = lax.dot_general(
            jnp.concatenate(weights, 1),
            jnp.concatenate(tents, 1),
            (((1,), (1,)), ((), ())),
            preferred_element_type=F32,
        )
        total = product if total is None else total + product
    total = total[:QT] + total[QT:]
    return (total[:, :CLS] + total[:, CLS:]) * scale


def kernel(
    lon_size,
    zonal_width,
    scale,
    v_hbm,
    t_hbm,
    bucket_hbm,
    slot_hbm,
    basin_hbm,
    lines_ref,
    numbers_ref,
    depth_ref,
    out_ref,
    v_ref,
    t_ref,
    bucket_ref,
    slot_ref,
    basin_ref,
    rows_ref,
    sums_ref,
    stats_ref,
    part_ref,
    core_ref,
    lons_ref,
    stats_send,
    stats_recv,
    core_send,
    core_recv,
    lon_send,
    lon_recv,
    last_send,
    last_recv,
    load_sems,
    done_ref,
    store_sems,
):
    levels, row_count, columns = v_ref.shape
    chunks = row_count // ROWS
    half = QT * CLS // 2
    lat = lax.axis_index("lat")
    lon = lax.axis_index("lon")
    lev = lax.axis_index("lev")
    other = 1 - lev
    mesh_id = pl.DeviceIdType.MESH

    pairs = (
        (basin_hbm, basin_ref),
        (v_hbm, v_ref),
        (t_hbm, t_ref),
        (bucket_hbm, bucket_ref),
        (slot_hbm, slot_ref),
    )
    loads = [pltpu.make_async_copy(a, b, load_sems.at[n]) for n, (a, b) in enumerate(pairs)]
    for load in loads:
        load.start()

    barrier = pltpu.get_barrier_semaphore()
    pl.semaphore_signal(barrier, inc=1, device_id={"lev": other}, device_id_type=mesh_id)
    for d in range(1, lon_size):
        pl.semaphore_signal(
            barrier, inc=1, device_id={"lon": lax.rem(lon + d, lon_size)}, device_id_type=mesh_id
        )

    for load in loads[:3]:
        load.wait()
    basin = basin_ref[...]
    lane = lax.broadcasted_iota(jnp.int32, (row_count, 128), 1)
    packed = jnp.zeros((row_count, 128), F32)
    for b in range(NB):
        mask = (basin == b).astype(F32)
        count = jnp.sum(mask, -1, keepdims=True)
        packed = jnp.where(lane == STATS * levels + b, count, packed)
        for k in range(levels):
            filtered = mask * v_ref[k]
            t = t_ref[k]
            for n, value in enumerate((filtered, mask * t, filtered * t)):
                total = jnp.sum(value, -1, keepdims=True)
                packed = jnp.where(lane == STATS * k + 2 * n + b, total, packed)
    stats_ref[lon] = packed

    pl.semaphore_wait(barrier, lon_size)

    def stats_copy(d):
        return pltpu.make_async_remote_copy(
            src_ref=stats_ref.at[lon],
            dst_ref=stats_ref.at[lon],
            send_sem=stats_send.at[d - 1],
            recv_sem=stats_recv.at[d - 1],
            device_id={"lon": lax.rem(lon + d, lon_size)},
            device_id_type=mesh_id,
        )

    for d in range(1, lon_size):
        stats_copy(d).start()

    numbers = numbers_ref[...]
    spot = (lax.broadcasted_iota(jnp.int32, numbers.shape, 0) == lon) & (
        lax.broadcasted_iota(jnp.int32, numbers.shape, 1) == lat
    )
    own = jnp.sum(jnp.where(spot, numbers.astype(F32), 0.0), -1, keepdims=True)
    own = jnp.sum(own, 0, keepdims=True)
    lines = lines_ref[...]
    square = (row_count, row_count)
    place = lax.broadcasted_iota(jnp.int32, square, 1).astype(F32)
    line = lax.broadcasted_iota(jnp.int32, square, 0)
    hit = jnp.where((line == lines) & (place < own), 1.0, 0.0)
    listed = jnp.max(hit, -1, keepdims=True)
    listed_basin = jnp.where(listed > 0.5, basin, NB)

    for load in loads[3:]:
        load.wait()
    for k in range(levels):
        prepare_classes(k, v_ref[k], t_ref[k], bucket_ref[k], slot_ref[k], listed_basin, rows_ref)

    for d in range(1, lon_size):
        stats_copy(d).wait()
    stats = stats_ref[0]
    for n in range(1, lon_size):
        stats = stats + stats_ref[n]

    depth = jnp.zeros((row_count, 128), F32)
    divisors = [
        jnp.maximum(stats[:, STATS * levels + b : STATS * levels + b + 1], 1.0) for b in range(NB)
    ]
    for k in range(levels):
        means = []
        for n in range(2):
            for b in range(NB):
                at = STATS * k + 2 * n + b
                means.append(stats[:, at : at + 1] / divisors[b])
        for b in range(NB):
            at = STATS * k + b
            overturning = stats[:, at : at + 1] * stats[:, at + 2 : at + 3] / divisors[b]
            eddy = (stats[:, at + 4 : at + 5] - overturning) / math.sqrt(zonal_width)
            depth = jnp.where(lane == b * levels + k, overturning, depth)
            depth = jnp.where(lane == (NB + b) * levels + k, eddy, depth)
        prepare_eddies(k, v_ref[k], t_ref[k], listed_basin, means, rows_ref)
    turned = depth.T
    for n in range(2):
        for b in range(NB):
            at = (n * NB + b) * levels
            depth_ref[n, b] = turned[at : at + levels]

    def core_copy(i):
        return pltpu.make_async_remote_copy(
            src_ref=part_ref.at[i, other],
            dst_ref=core_ref.at[i],
            send_sem=core_send.at[i],
            recv_sem=core_recv.at[i],
            device_id={"lev": other},
            device_id_type=mesh_id,
        )

    def lon_copy(i, d):
        return pltpu.make_async_remote_copy(
            src_ref=lons_ref.at[lon, i],
            dst_ref=lons_ref.at[lon, i],
            send_sem=lon_send.at[i, d - 1],
            recv_sem=lon_recv.at[i, d - 1],
            device_id={"lon": lax.rem(lon + d, lon_size)},
            device_id_type=mesh_id,
        )

    def out_block(i):
        rows = pl.ds(pl.multiple_of(i * ROWS, ROWS), ROWS)
        return done_ref.at[rows, pl.ds(pl.multiple_of(lev * half, 128), half)]

    def last_copy(i):
        return pltpu.make_async_remote_copy(
            src_ref=out_block(i),
            dst_ref=out_block(i),
            send_sem=last_send.at[i],
            recv_sem=last_recv.at[i],
            device_id={"lev": other},
            device_id_type=mesh_id,
        )

    def store(i):
        rows = pl.ds(pl.multiple_of(i * ROWS, ROWS), ROWS)
        return pltpu.make_async_copy(done_ref.at[rows], out_ref.at[rows], store_sems.at[i])

    def give(i):
        last_copy(i).wait_recv()
        store(i).start()

    def over_cores(i):
        core_copy(i).wait_recv()
        lons_ref[lon, i] = part_ref[i, lev] + core_ref[i]
        for d in range(1, lon_size):
            lon_copy(i, d).start()

    def over_lons(i):
        for d in range(1, lon_size):
            lon_copy(i, d).wait_recv()
        total = lons_ref[0, i]
        for n in range(1, lon_size):
            total = total + lons_ref[n, i]
        out_block(i)[...] = total
        last_copy(i).start()

    def one_chunk(i, carry):
        def some_rows(step, inner):
            for u in range(UNROLL):
                r = step * UNROLL + u
                binned = bin_row(i * ROWS + r, rows_ref, levels, columns, scale)
                binned = jnp.concatenate([binned, jnp.zeros((QT, 128 - CLS), F32)], 1)
                sums_ref[pl.ds(r, QT, stride=ROWS), :] = binned
            return inner

        lax.fori_loop(0, ROWS // UNROLL, some_rows, 0)

        for m in range(0, QT, 4):
            parts = [sums_ref[(m + n) * ROWS : (m + n + 1) * ROWS, :][:, :CLS] for n in range(4)]
            h, at = divmod(m * CLS, half)
            part_ref[i, h, :, at : at + 4 * CLS] = jnp.concatenate(parts, 1)
        core_copy(i).start()

        @pl.when(i >= 2)
        def _():
            give(i - 2)

        @pl.when(i >= 1)
        def _():
            over_lons(i - 1)

        over_cores(i)
        return carry

    lax.fori_loop(0, chunks, one_chunk, 0)
    if chunks >= 2:
        give(chunks - 2)
    over_lons(chunks - 1)
    give(chunks - 1)

    def finish(i, carry):
        core_copy(i).wait_send()
        for d in range(1, lon_size):
            lon_copy(i, d).wait_send()
        last_copy(i).wait_send()
        store(i).wait()
        return carry

    lax.fori_loop(0, chunks, finish, 0)


def shards(
    northward_speed,
    thermal_anomaly,
    isopycnal_bucket,
    isopycnal_bucket_slot,
    profile_region_number,
    partition_sea_lines,
    partition_sea_numbers,
):
    levels, row_count, columns = northward_speed.shape
    lon_size = lax.axis_size("lon")
    zonal_width = columns * lon_size
    level_count = levels * lax.axis_size("lev")
    chunks = row_count // ROWS
    half = QT * CLS // 2
    scale = 1.0 / math.sqrt(level_count * zonal_width / (CLS * TCLS))
    vmem = pl.BlockSpec(memory_space=pltpu.VMEM)
    dma = pltpu.SemaphoreType.DMA
    return pl.pallas_call(
        functools.partial(kernel, lon_size, zonal_width, scale),
        out_shape=(
            jax.ShapeDtypeStruct((2, NB, levels, row_count), F32),
            jax.ShapeDtypeStruct((row_count, QT * CLS), F32),
        ),
        in_specs=[pl.BlockSpec(memory_space=pl.ANY)] * 5 + [vmem] * 2,
        out_specs=(vmem, pl.BlockSpec(memory_space=pl.ANY)),
        scratch_shapes=[
            pltpu.VMEM((levels, row_count, columns), F32),
            pltpu.VMEM((levels, row_count, columns), F32),
            pltpu.VMEM((levels, row_count, columns), jnp.int32),
            pltpu.VMEM((levels, row_count, columns), F32),
            pltpu.VMEM((row_count, columns), jnp.int32),
            pltpu.VMEM((14, levels, row_count, columns), F32),
            pltpu.VMEM((QT * ROWS, 128), F32),
            pltpu.VMEM((lon_size, row_count, 128), F32),
            pltpu.VMEM((chunks, 2, ROWS, half), F32),
            pltpu.VMEM((chunks, ROWS, half), F32),
            pltpu.VMEM((lon_size, chunks, ROWS, half), F32),
            dma((lon_size - 1,)),
            dma((lon_size - 1,)),
            dma((chunks,)),
            dma((chunks,)),
            dma((chunks, lon_size - 1)),
            dma((chunks, lon_size - 1)),
            dma((chunks,)),
            dma((chunks,)),
            dma((5,)),
            pltpu.VMEM((row_count, QT * CLS), F32),
            dma((chunks,)),
        ],
        compiler_params=pltpu.CompilerParams(
            collective_id=0, has_side_effects=True, vmem_limit_bytes=60 * 1024 * 1024
        ),
    )(
        northward_speed,
        thermal_anomaly,
        isopycnal_bucket,
        isopycnal_bucket_slot,
        profile_region_number,
        partition_sea_lines.reshape(1, row_count),
        partition_sea_numbers.T,
    )


def solution(mesh):
    in_specs = (
        P(("runs", "lev"), "lat", "lon"),
        P(("runs", "lev"), "lat", "lon"),
        P(("runs", "lev"), "lat", "lon"),
        P(("runs", "lev"), "lat", "lon"),
        P(("runs", "lat"), "lon"),
        P(("runs", "lat"), "lon", None),
        P("runs", None),
    )
    out_specs = (P("runs", None, "lev", "lat"), P(("runs", "lat"), None))
    return jax.shard_map(shards, mesh=mesh, in_specs=in_specs, out_specs=out_specs, check_vma=False)
```

```python
import functools
import math

import jax
import jax.numpy as jnp
from jax import lax
from jax.experimental import pallas as pl
from jax.experimental.pallas import tpu as pltpu
from jax.sharding import PartitionSpec as P

CLS = 96
TCLS = 32
NB = 2
BT = NB * TCLS
QT = 2 * BT
F32 = jnp.float32
BF16 = jnp.bfloat16


def split(x):
    high = x.astype(BF16).astype(F32)
    return high, x - high


ROWS = 8
STATS = 8
UNROLL = 4
PIECES = 4


def temperature(t):
    temp_pos = jnp.minimum(jnp.maximum((t + 3.0) * (TCLS / 6.0), 0.0), TCLS - 1.0)
    temp = jnp.floor(temp_pos)
    return temp, temp_pos - temp


def prepare_classes(k, v, t, bucket, slot, listed_basin, rows_ref):
    position = jnp.minimum(bucket.astype(F32) + slot, CLS - 1.0)
    cls = jnp.floor(position)
    upper = position - cls
    temp, warm = temperature(t)
    joint = jnp.where(
        listed_basin == 0, temp, jnp.where(listed_basin == 1, temp + TCLS, -128.0)
    )
    values = [cls, *split(1.0 - upper), *split(upper), joint]
    values += [*split(v * (1.0 - warm)), *split(v * warm)]
    for at, value in enumerate(values):
        rows_ref[at, k] = value


def prepare_eddies(k, v, t, listed_basin, means, rows_ref):
    first = listed_basin == 0
    eddy = (v - jnp.where(first, means[0], means[1])) * (t - jnp.where(first, means[2], means[3]))
    _, warm = temperature(t)
    for at, value in enumerate([*split(eddy * (1.0 - warm)), *split(eddy * warm)]):
        rows_ref[10 + at, k] = value


def bin_row(y, rows_ref, levels, columns, scale):
    spots = lax.broadcasted_iota(jnp.int32, (16, columns), 0).astype(F32)
    total = None
    step = 2 if levels % 2 == 0 else 1
    for k0 in range(0, levels, step):
        tents, weights = [], []
        for k in range(k0, k0 + step):
            def row(at):
                return jnp.broadcast_to(rows_ref[at, k, pl.ds(y, 1), :], (16, columns)).astype(BF16)

            zero = jnp.zeros((16, columns), BF16)
            cls, low_hi, low_lo, up_hi, up_lo, joint = [row(at) for at in range(6)]
            feats = [row(at) for at in range(6, 14)]
            tent_hi, tent_lo = [], []
            for c in range(0, CLS, 16):
                here = (spots + float(c)).astype(BF16)
                before = (spots + float(c - 1)).astype(BF16)
                at_low = cls == here
                at_up = cls == before
                tent_hi.append(jnp.where(at_low, low_hi, jnp.where(at_up, up_hi, zero)))
                tent_lo.append(jnp.where(at_low, low_lo, jnp.where(at_up, up_lo, zero)))
            blocks = [[], [], [], []]
            for c in range(0, BT, 16):
                here = (spots + float(c)).astype(BF16)
                before = (spots + float(c - 1)).astype(BF16)
                at_low = joint == here
                at_up = joint == before
                for n, (kind, part) in enumerate(((0, 0), (1, 0), (0, 1), (1, 1))):
                    low = feats[4 * kind + part]
                    up = feats[4 * kind + 2 + part]
                    blocks[n].append(jnp.where(at_low, low, jnp.where(at_up, up, zero)))
            tents.append(jnp.concatenate(tent_hi + tent_lo, 0))
            weights.append(jnp.concatenate(sum(blocks, []), 0))
        product = lax.dot_general(
            jnp.concatenate(weights, 1),
            jnp.concatenate(tents, 1),
            (((1,), (1,)), ((), ())),
            preferred_element_type=F32,
        )
        total = product if total is None else total + product
    total = total[:QT] + total[QT:]
    return (total[:, :CLS] + total[:, CLS:]) * scale


def kernel(
    lon_size,
    zonal_width,
    scale,
    v_hbm,
    t_hbm,
    bucket_hbm,
    slot_hbm,
    basin_hbm,
    lines_ref,
    numbers_ref,
    depth_ref,
    out_ref,
    v_ref,
    t_ref,
    bucket_ref,
    slot_ref,
    basin_ref,
    rows_ref,
    sums_ref,
    stats_ref,
    part_ref,
    core_ref,
    lons_ref,
    stats_send,
    stats_recv,
    core_send,
    core_recv,
    lon_send,
    lon_recv,
    last_send,
    last_recv,
    load_sems,
):
    levels, row_count, columns = v_ref.shape
    chunks = row_count // ROWS
    half = QT * CLS // 2
    lat = lax.axis_index("lat")
    lon = lax.axis_index("lon")
    lev = lax.axis_index("lev")
    other = 1 - lev
    mesh_id = pl.DeviceIdType.MESH

    pairs = (
        (basin_hbm, basin_ref),
        (v_hbm, v_ref),
        (t_hbm, t_ref),
        (bucket_hbm, bucket_ref),
        (slot_hbm, slot_ref),
    )
    loads = [pltpu.make_async_copy(a, b, load_sems.at[n]) for n, (a, b) in enumerate(pairs)]
    for load in loads:
        load.start()

    barrier = pltpu.get_barrier_semaphore()
    pl.semaphore_signal(barrier, inc=1, device_id={"lev": other}, device_id_type=mesh_id)
    for d in range(1, lon_size):
        pl.semaphore_signal(
            barrier, inc=1, device_id={"lon": lax.rem(lon + d, lon_size)}, device_id_type=mesh_id
        )

    for load in loads[:3]:
        load.wait()
    basin = basin_ref[...]
    lane = lax.broadcasted_iota(jnp.int32, (row_count, 128), 1)
    packed = jnp.zeros((row_count, 128), F32)
    for b in range(NB):
        mask = (basin == b).astype(F32)
        count = jnp.sum(mask, -1, keepdims=True)
        packed = jnp.where(lane == STATS * levels + b, count, packed)
        for k in range(levels):
            filtered = mask * v_ref[k]
            t = t_ref[k]
            for n, value in enumerate((filtered, mask * t, filtered * t)):
                total = jnp.sum(value, -1, keepdims=True)
                packed = jnp.where(lane == STATS * k + 2 * n + b, total, packed)
    stats_ref[lon] = packed

    pl.semaphore_wait(barrier, lon_size)

    def stats_copy(d):
        return pltpu.make_async_remote_copy(
            src_ref=stats_ref.at[lon],
            dst_ref=stats_ref.at[lon],
            send_sem=stats_send.at[d - 1],
            recv_sem=stats_recv.at[d - 1],
            device_id={"lon": lax.rem(lon + d, lon_size)},
            device_id_type=mesh_id,
        )

    for d in range(1, lon_size):
        stats_copy(d).start()

    numbers = numbers_ref[...]
    spot = (lax.broadcasted_iota(jnp.int32, numbers.shape, 0) == lon) & (
        lax.broadcasted_iota(jnp.int32, numbers.shape, 1) == lat
    )
    own = jnp.sum(jnp.where(spot, numbers.astype(F32), 0.0), -1, keepdims=True)
    own = jnp.sum(own, 0, keepdims=True)
    lines = lines_ref[...]
    square = (row_count, row_count)
    place = lax.broadcasted_iota(jnp.int32, square, 1).astype(F32)
    line = lax.broadcasted_iota(jnp.int32, square, 0)
    hit = jnp.where((line == lines) & (place < own), 1.0, 0.0)
    listed = jnp.max(hit, -1, keepdims=True)
    listed_basin = jnp.where(listed > 0.5, basin, NB)

    for load in loads[3:]:
        load.wait()
    for k in range(levels):
        prepare_classes(k, v_ref[k], t_ref[k], bucket_ref[k], slot_ref[k], listed_basin, rows_ref)

    for d in range(1, lon_size):
        stats_copy(d).wait()
    stats = stats_ref[0]
    for n in range(1, lon_size):
        stats = stats + stats_ref[n]

    depth = jnp.zeros((row_count, 128), F32)
    divisors = [
        jnp.maximum(stats[:, STATS * levels + b : STATS * levels + b + 1], 1.0) for b in range(NB)
    ]
    for k in range(levels):
        means = []
        for n in range(2):
            for b in range(NB):
                at = STATS * k + 2 * n + b
                means.append(stats[:, at : at + 1] / divisors[b])
        for b in range(NB):
            at = STATS * k + b
            overturning = stats[:, at : at + 1] * stats[:, at + 2 : at + 3] / divisors[b]
            eddy = (stats[:, at + 4 : at + 5] - overturning) / math.sqrt(zonal_width)
            depth = jnp.where(lane == b * levels + k, overturning, depth)
            depth = jnp.where(lane == (NB + b) * levels + k, eddy, depth)
        prepare_eddies(k, v_ref[k], t_ref[k], listed_basin, means, rows_ref)
    turned = depth.T
    for n in range(2):
        for b in range(NB):
            at = (n * NB + b) * levels
            depth_ref[n, b] = turned[at : at + levels]

    width = half // PIECES

    def core_copy(i, p):
        lanes = pl.ds(p * width, width)
        return pltpu.make_async_remote_copy(
            src_ref=part_ref.at[i, other, :, lanes],
            dst_ref=core_ref.at[i, :, lanes],
            send_sem=core_send.at[i, p],
            recv_sem=core_recv.at[i, p],
            device_id={"lev": other},
            device_id_type=mesh_id,
        )

    def lon_copy(i, p, d):
        block = lons_ref.at[lon, i, :, pl.ds(p * width, width)]
        return pltpu.make_async_remote_copy(
            src_ref=block,
            dst_ref=block,
            send_sem=lon_send.at[i, p, d - 1],
            recv_sem=lon_recv.at[i, p, d - 1],
            device_id={"lon": lax.rem(lon + d, lon_size)},
            device_id_type=mesh_id,
        )

    def out_block(i, p):
        rows = pl.ds(pl.multiple_of(i * ROWS, ROWS), ROWS)
        return out_ref.at[rows, pl.ds(pl.multiple_of(lev * half + p * width, 128), width)]

    def last_copy(i, p):
        return pltpu.make_async_remote_copy(
            src_ref=out_block(i, p),
            dst_ref=out_block(i, p),
            send_sem=last_send.at[i, p],
            recv_sem=last_recv.at[i, p],
            device_id={"lev": other},
            device_id_type=mesh_id,
        )

    def over_cores(i):
        for p in range(PIECES):
            lanes = slice(p * width, (p + 1) * width)
            core_copy(i, p).wait_recv()
            lons_ref[lon, i, :, lanes] = part_ref[i, lev, :, lanes] + core_ref[i, :, lanes]
            for d in range(1, lon_size):
                lon_copy(i, p, d).start()

    def over_lons(i):
        for p in range(PIECES):
            lanes = slice(p * width, (p + 1) * width)
            for d in range(1, lon_size):
                lon_copy(i, p, d).wait_recv()
            total = lons_ref[0, i, :, lanes]
            for n in range(1, lon_size):
                total = total + lons_ref[n, i, :, lanes]
            out_block(i, p)[...] = total
            last_copy(i, p).start()

    def one_chunk(i, carry):
        def some_rows(step, inner):
            for u in range(UNROLL):
                r = step * UNROLL + u
                binned = bin_row(i * ROWS + r, rows_ref, levels, columns, scale)
                binned = jnp.concatenate([binned, jnp.zeros((QT, 128 - CLS), F32)], 1)
                sums_ref[pl.ds(r, QT, stride=ROWS), :] = binned
            return inner

        lax.fori_loop(0, ROWS // UNROLL, some_rows, 0)

        for p in range(PIECES):
            for h in range(2):
                for m in range(p * (QT // 2 // PIECES), (p + 1) * (QT // 2 // PIECES), 4):
                    first = (h * (QT // 2) + m) * ROWS
                    parts = [
                        sums_ref[first + n * ROWS : first + (n + 1) * ROWS, :][:, :CLS]
                        for n in range(4)
                    ]
                    part_ref[i, h, :, m * CLS : (m + 4) * CLS] = jnp.concatenate(parts, 1)
            core_copy(i, p).start()

        @pl.when(i >= 1)
        def _():
            over_lons(i - 1)

        over_cores(i)
        return carry

    lax.fori_loop(0, chunks, one_chunk, 0)
    over_lons(chunks - 1)

    def finish(i, carry):
        for p in range(PIECES):
            core_copy(i, p).wait_send()
            for d in range(1, lon_size):
                lon_copy(i, p, d).wait_send()
            last_copy(i, p).wait()
        return carry

    lax.fori_loop(0, chunks, finish, 0)


def shards(
    northward_speed,
    thermal_anomaly,
    isopycnal_bucket,
    isopycnal_bucket_slot,
    profile_region_number,
    partition_sea_lines,
    partition_sea_numbers,
):
    levels, row_count, columns = northward_speed.shape
    lon_size = lax.axis_size("lon")
    zonal_width = columns * lon_size
    level_count = levels * lax.axis_size("lev")
    chunks = row_count // ROWS
    half = QT * CLS // 2
    scale = 1.0 / math.sqrt(level_count * zonal_width / (CLS * TCLS))
    vmem = pl.BlockSpec(memory_space=pltpu.VMEM)
    dma = pltpu.SemaphoreType.DMA
    return pl.pallas_call(
        functools.partial(kernel, lon_size, zonal_width, scale),
        out_shape=(
            pltpu.VMEM((2, NB, levels, row_count), F32),
            pltpu.VMEM((row_count, QT * CLS), F32),
        ),
        in_specs=[pl.BlockSpec(memory_space=pl.ANY)] * 5 + [vmem] * 2,
        out_specs=(vmem, vmem),
        scratch_shapes=[
            pltpu.VMEM((levels, row_count, columns), F32),
            pltpu.VMEM((levels, row_count, columns), F32),
            pltpu.VMEM((levels, row_count, columns), jnp.int32),
            pltpu.VMEM((levels, row_count, columns), F32),
            pltpu.VMEM((row_count, columns), jnp.int32),
            pltpu.VMEM((14, levels, row_count, columns), F32),
            pltpu.VMEM((QT * ROWS, 128), F32),
            pltpu.VMEM((lon_size, row_count, 128), F32),
            pltpu.VMEM((chunks, 2, ROWS, half), F32),
            pltpu.VMEM((chunks, ROWS, half), F32),
            pltpu.VMEM((lon_size, chunks, ROWS, half), F32),
            dma((lon_size - 1,)),
            dma((lon_size - 1,)),
            dma((chunks, PIECES)),
            dma((chunks, PIECES)),
            dma((chunks, PIECES, lon_size - 1)),
            dma((chunks, PIECES, lon_size - 1)),
            dma((chunks, PIECES)),
            dma((chunks, PIECES)),
            dma((5,)),
        ],
        compiler_params=pltpu.CompilerParams(
            collective_id=0, has_side_effects=True, vmem_limit_bytes=60 * 1024 * 1024
        ),
    )(
        northward_speed,
        thermal_anomaly,
        isopycnal_bucket,
        isopycnal_bucket_slot,
        profile_region_number,
        partition_sea_lines.reshape(1, row_count),
        partition_sea_numbers.T,
    )


def solution(mesh):
    in_specs = (
        P(("runs", "lev"), "lat", "lon"),
        P(("runs", "lev"), "lat", "lon"),
        P(("runs", "lev"), "lat", "lon"),
        P(("runs", "lev"), "lat", "lon"),
        P(("runs", "lat"), "lon"),
        P(("runs", "lat"), "lon", None),
        P("runs", None),
    )
    out_specs = (P("runs", None, "lev", "lat"), P(("runs", "lat"), None))
    return jax.shard_map(shards, mesh=mesh, in_specs=in_specs, out_specs=out_specs, check_vma=False)
```

```python
import functools
import math

import jax
import jax.numpy as jnp
from jax import lax
from jax.experimental import pallas as pl
from jax.experimental.pallas import tpu as pltpu
from jax.sharding import PartitionSpec as P

CLS = 96
TCLS = 32
NB = 2
BT = NB * TCLS
QT = 2 * BT
F32 = jnp.float32
BF16 = jnp.bfloat16


def split(x):
    high = x.astype(BF16).astype(F32)
    return high, x - high


ROWS = 8
STATS = 8
UNROLL = 8
PIECES = 4


def temperature(t):
    temp_pos = jnp.minimum(jnp.maximum((t + 3.0) * (TCLS / 6.0), 0.0), TCLS - 1.0)
    temp = jnp.floor(temp_pos)
    return temp, temp_pos - temp


def prepare_classes(k, v, t, bucket, slot, listed_basin, rows_ref):
    position = jnp.minimum(bucket.astype(F32) + slot, CLS - 1.0)
    cls = jnp.floor(position)
    upper = position - cls
    temp, warm = temperature(t)
    joint = jnp.where(
        listed_basin == 0, temp, jnp.where(listed_basin == 1, temp + TCLS, -128.0)
    )
    values = [cls, *split(1.0 - upper), *split(upper), joint]
    values += [*split(v * (1.0 - warm)), *split(v * warm)]
    for at, value in enumerate(values):
        rows_ref[at, k] = value


def prepare_eddies(k, v, t, listed_basin, means, rows_ref):
    first = listed_basin == 0
    eddy = (v - jnp.where(first, means[0], means[1])) * (t - jnp.where(first, means[2], means[3]))
    _, warm = temperature(t)
    for at, value in enumerate([*split(eddy * (1.0 - warm)), *split(eddy * warm)]):
        rows_ref[10 + at, k] = value


def bin_row(y, rows_ref, levels, columns, scale):
    spots = lax.broadcasted_iota(jnp.int32, (16, columns), 0).astype(F32)
    total = None
    step = 2 if levels % 2 == 0 else 1
    for k0 in range(0, levels, step):
        tents, weights = [], []
        for k in range(k0, k0 + step):
            def row(at):
                return jnp.broadcast_to(rows_ref[at, k, pl.ds(y, 1), :], (16, columns)).astype(BF16)

            zero = jnp.zeros((16, columns), BF16)
            cls, low_hi, low_lo, up_hi, up_lo, joint = [row(at) for at in range(6)]
            feats = [row(at) for at in range(6, 14)]
            tent_hi, tent_lo = [], []
            for c in range(0, CLS, 16):
                here = (spots + float(c)).astype(BF16)
                before = (spots + float(c - 1)).astype(BF16)
                at_low = cls == here
                at_up = cls == before
                tent_hi.append(jnp.where(at_low, low_hi, jnp.where(at_up, up_hi, zero)))
                tent_lo.append(jnp.where(at_low, low_lo, jnp.where(at_up, up_lo, zero)))
            blocks = [[], [], [], []]
            for c in range(0, BT, 16):
                here = (spots + float(c)).astype(BF16)
                before = (spots + float(c - 1)).astype(BF16)
                at_low = joint == here
                at_up = joint == before
                for n, (kind, part) in enumerate(((0, 0), (1, 0), (0, 1), (1, 1))):
                    low = feats[4 * kind + part]
                    up = feats[4 * kind + 2 + part]
                    blocks[n].append(jnp.where(at_low, low, jnp.where(at_up, up, zero)))
            tents.append(jnp.concatenate(tent_hi + tent_lo, 0))
            weights.append(jnp.concatenate(sum(blocks, []), 0))
        product = lax.dot_general(
            jnp.concatenate(weights, 1),
            jnp.concatenate(tents, 1),
            (((1,), (1,)), ((), ())),
            preferred_element_type=F32,
        )
        total = product if total is None else total + product
    total = total[:QT] + total[QT:]
    return (total[:, :CLS] + total[:, CLS:]) * scale


def kernel(
    lon_size,
    zonal_width,
    scale,
    v_hbm,
    t_hbm,
    bucket_hbm,
    slot_hbm,
    basin_hbm,
    lines_ref,
    numbers_ref,
    depth_ref,
    out_ref,
    v_ref,
    t_ref,
    bucket_ref,
    slot_ref,
    basin_ref,
    rows_ref,
    sums_ref,
    stats_ref,
    part_ref,
    core_ref,
    lons_ref,
    stats_send,
    stats_recv,
    core_send,
    core_recv,
    lon_send,
    lon_recv,
    last_send,
    last_recv,
    load_sems,
):
    levels, row_count, columns = v_ref.shape
    chunks = row_count // ROWS
    half = QT * CLS // 2
    lat = lax.axis_index("lat")
    lon = lax.axis_index("lon")
    lev = lax.axis_index("lev")
    other = 1 - lev
    mesh_id = pl.DeviceIdType.MESH

    pairs = (
        (basin_hbm, basin_ref),
        (v_hbm, v_ref),
        (t_hbm, t_ref),
        (bucket_hbm, bucket_ref),
        (slot_hbm, slot_ref),
    )
    loads = [pltpu.make_async_copy(a, b, load_sems.at[n]) for n, (a, b) in enumerate(pairs)]
    for load in loads:
        load.start()

    barrier = pltpu.get_barrier_semaphore()
    pl.semaphore_signal(barrier, inc=1, device_id={"lev": other}, device_id_type=mesh_id)
    for d in range(1, lon_size):
        pl.semaphore_signal(
            barrier, inc=1, device_id={"lon": lax.rem(lon + d, lon_size)}, device_id_type=mesh_id
        )

    for load in loads[:3]:
        load.wait()
    basin = basin_ref[...]
    lane = lax.broadcasted_iota(jnp.int32, (row_count, 128), 1)
    packed = jnp.zeros((row_count, 128), F32)
    for b in range(NB):
        mask = (basin == b).astype(F32)
        count = jnp.sum(mask, -1, keepdims=True)
        packed = jnp.where(lane == STATS * levels + b, count, packed)
        for k in range(levels):
            filtered = mask * v_ref[k]
            t = t_ref[k]
            for n, value in enumerate((filtered, mask * t, filtered * t)):
                total = jnp.sum(value, -1, keepdims=True)
                packed = jnp.where(lane == STATS * k + 2 * n + b, total, packed)
    stats_ref[lon] = packed

    pl.semaphore_wait(barrier, lon_size)

    def stats_copy(d):
        return pltpu.make_async_remote_copy(
            src_ref=stats_ref.at[lon],
            dst_ref=stats_ref.at[lon],
            send_sem=stats_send.at[d - 1],
            recv_sem=stats_recv.at[d - 1],
            device_id={"lon": lax.rem(lon + d, lon_size)},
            device_id_type=mesh_id,
        )

    for d in range(1, lon_size):
        stats_copy(d).start()

    numbers = numbers_ref[...]
    spot = (lax.broadcasted_iota(jnp.int32, numbers.shape, 0) == lon) & (
        lax.broadcasted_iota(jnp.int32, numbers.shape, 1) == lat
    )
    own = jnp.sum(jnp.where(spot, numbers.astype(F32), 0.0), -1, keepdims=True)
    own = jnp.sum(own, 0, keepdims=True)
    lines = lines_ref[...]
    square = (row_count, row_count)
    place = lax.broadcasted_iota(jnp.int32, square, 1).astype(F32)
    line = lax.broadcasted_iota(jnp.int32, square, 0)
    hit = jnp.where((line == lines) & (place < own), 1.0, 0.0)
    listed = jnp.max(hit, -1, keepdims=True)
    listed_basin = jnp.where(listed > 0.5, basin, NB)

    for load in loads[3:]:
        load.wait()
    for k in range(levels):
        prepare_classes(k, v_ref[k], t_ref[k], bucket_ref[k], slot_ref[k], listed_basin, rows_ref)

    for d in range(1, lon_size):
        stats_copy(d).wait()
    stats = stats_ref[0]
    for n in range(1, lon_size):
        stats = stats + stats_ref[n]

    depth = jnp.zeros((row_count, 128), F32)
    divisors = [
        jnp.maximum(stats[:, STATS * levels + b : STATS * levels + b + 1], 1.0) for b in range(NB)
    ]
    for k in range(levels):
        means = []
        for n in range(2):
            for b in range(NB):
                at = STATS * k + 2 * n + b
                means.append(stats[:, at : at + 1] / divisors[b])
        for b in range(NB):
            at = STATS * k + b
            overturning = stats[:, at : at + 1] * stats[:, at + 2 : at + 3] / divisors[b]
            eddy = (stats[:, at + 4 : at + 5] - overturning) / math.sqrt(zonal_width)
            depth = jnp.where(lane == b * levels + k, overturning, depth)
            depth = jnp.where(lane == (NB + b) * levels + k, eddy, depth)
        prepare_eddies(k, v_ref[k], t_ref[k], listed_basin, means, rows_ref)
    turned = depth.T
    for n in range(2):
        for b in range(NB):
            at = (n * NB + b) * levels
            depth_ref[n, b] = turned[at : at + levels]

    width = half // PIECES

    def core_copy(i, p):
        lanes = pl.ds(p * width, width)
        return pltpu.make_async_remote_copy(
            src_ref=part_ref.at[i, other, :, lanes],
            dst_ref=core_ref.at[i, :, lanes],
            send_sem=core_send.at[i, p],
            recv_sem=core_recv.at[i, p],
            device_id={"lev": other},
            device_id_type=mesh_id,
        )

    def lon_copy(i, p, d):
        block = lons_ref.at[lon, i, :, pl.ds(p * width, width)]
        return pltpu.make_async_remote_copy(
            src_ref=block,
            dst_ref=block,
            send_sem=lon_send.at[i, p, d - 1],
            recv_sem=lon_recv.at[i, p, d - 1],
            device_id={"lon": lax.rem(lon + d, lon_size)},
            device_id_type=mesh_id,
        )

    def out_block(i, p):
        rows = pl.ds(pl.multiple_of(i * ROWS, ROWS), ROWS)
        return out_ref.at[rows, pl.ds(pl.multiple_of(lev * half + p * width, 128), width)]

    def last_copy(i, p):
        return pltpu.make_async_remote_copy(
            src_ref=out_block(i, p),
            dst_ref=out_block(i, p),
            send_sem=last_send.at[i, p],
            recv_sem=last_recv.at[i, p],
            device_id={"lev": other},
            device_id_type=mesh_id,
        )

    def over_cores(i):
        for p in range(PIECES):
            lanes = slice(p * width, (p + 1) * width)
            core_copy(i, p).wait_recv()
            lons_ref[lon, i, :, lanes] = part_ref[i, lev, :, lanes] + core_ref[i, :, lanes]
            for d in range(1, lon_size):
                lon_copy(i, p, d).start()

    def over_lons(i):
        for p in range(PIECES):
            lanes = slice(p * width, (p + 1) * width)
            for d in range(1, lon_size):
                lon_copy(i, p, d).wait_recv()
            total = lons_ref[0, i, :, lanes]
            for n in range(1, lon_size):
                total = total + lons_ref[n, i, :, lanes]
            out_block(i, p)[...] = total
            last_copy(i, p).start()

    def one_chunk(i, carry):
        def some_rows(step, inner):
            for u in range(UNROLL):
                r = step * UNROLL + u
                binned = bin_row(i * ROWS + r, rows_ref, levels, columns, scale)
                binned = jnp.concatenate([binned, jnp.zeros((QT, 128 - CLS), F32)], 1)
                sums_ref[pl.ds(r, QT, stride=ROWS), :] = binned
            return inner

        lax.fori_loop(0, ROWS // UNROLL, some_rows, 0)

        for p in range(PIECES):
            for h in range(2):
                for m in range(p * (QT // 2 // PIECES), (p + 1) * (QT // 2 // PIECES), 4):
                    first = (h * (QT // 2) + m) * ROWS
                    parts = [
                        sums_ref[first + n * ROWS : first + (n + 1) * ROWS, :][:, :CLS]
                        for n in range(4)
                    ]
                    part_ref[i, h, :, m * CLS : (m + 4) * CLS] = jnp.concatenate(parts, 1)
            core_copy(i, p).start()

        @pl.when(i >= 1)
        def _():
            over_lons(i - 1)

        over_cores(i)
        return carry

    lax.fori_loop(0, chunks, one_chunk, 0)
    over_lons(chunks - 1)

    def finish(i, carry):
        for p in range(PIECES):
            core_copy(i, p).wait_send()
            for d in range(1, lon_size):
                lon_copy(i, p, d).wait_send()
            last_copy(i, p).wait()
        return carry

    lax.fori_loop(0, chunks, finish, 0)


def shards(
    northward_speed,
    thermal_anomaly,
    isopycnal_bucket,
    isopycnal_bucket_slot,
    profile_region_number,
    partition_sea_lines,
    partition_sea_numbers,
):
    levels, row_count, columns = northward_speed.shape
    lon_size = lax.axis_size("lon")
    zonal_width = columns * lon_size
    level_count = levels * lax.axis_size("lev")
    chunks = row_count // ROWS
    half = QT * CLS // 2
    scale = 1.0 / math.sqrt(level_count * zonal_width / (CLS * TCLS))
    vmem = pl.BlockSpec(memory_space=pltpu.VMEM)
    dma = pltpu.SemaphoreType.DMA
    return pl.pallas_call(
        functools.partial(kernel, lon_size, zonal_width, scale),
        out_shape=(
            pltpu.VMEM((2, NB, levels, row_count), F32),
            pltpu.VMEM((row_count, QT * CLS), F32),
        ),
        in_specs=[pl.BlockSpec(memory_space=pl.ANY)] * 5 + [vmem] * 2,
        out_specs=(vmem, vmem),
        scratch_shapes=[
            pltpu.VMEM((levels, row_count, columns), F32),
            pltpu.VMEM((levels, row_count, columns), F32),
            pltpu.VMEM((levels, row_count, columns), jnp.int32),
            pltpu.VMEM((levels, row_count, columns), F32),
            pltpu.VMEM((row_count, columns), jnp.int32),
            pltpu.VMEM((14, levels, row_count, columns), F32),
            pltpu.VMEM((QT * ROWS, 128), F32),
            pltpu.VMEM((lon_size, row_count, 128), F32),
            pltpu.VMEM((chunks, 2, ROWS, half), F32),
            pltpu.VMEM((chunks, ROWS, half), F32),
            pltpu.VMEM((lon_size, chunks, ROWS, half), F32),
            dma((lon_size - 1,)),
            dma((lon_size - 1,)),
            dma((chunks, PIECES)),
            dma((chunks, PIECES)),
            dma((chunks, PIECES, lon_size - 1)),
            dma((chunks, PIECES, lon_size - 1)),
            dma((chunks, PIECES)),
            dma((chunks, PIECES)),
            dma((5,)),
        ],
        compiler_params=pltpu.CompilerParams(
            collective_id=0, has_side_effects=True, vmem_limit_bytes=60 * 1024 * 1024
        ),
    )(
        northward_speed,
        thermal_anomaly,
        isopycnal_bucket,
        isopycnal_bucket_slot,
        profile_region_number,
        partition_sea_lines.reshape(1, row_count),
        partition_sea_numbers.T,
    )


def solution(mesh):
    in_specs = (
        P(("runs", "lev"), "lat", "lon"),
        P(("runs", "lev"), "lat", "lon"),
        P(("runs", "lev"), "lat", "lon"),
        P(("runs", "lev"), "lat", "lon"),
        P(("runs", "lat"), "lon"),
        P(("runs", "lat"), "lon", None),
        P("runs", None),
    )
    out_specs = (P("runs", None, "lev", "lat"), P(("runs", "lat"), None))
    return jax.shard_map(shards, mesh=mesh, in_specs=in_specs, out_specs=out_specs, check_vma=False)
```
